256 devices in a mesh: lon: 32 (over z, y_hi, core), lat: 8 (over y_lo, x).
Axes of the slice: x: 4, y: 4 (y_hi: 2, y_lo: 2; y = y_hi * 2 + y_lo), z: 8, core: 2. Of those that a mesh axis runs over, the one named last changes fastest.
Arguments:
- features: bfloat16 [65536, 512], P(('lon', 'lat')), may hold values from -6 to 6
- cotangent: bfloat16 [65536, 512], P(('lon', 'lat')), may hold values from -6 to 6
- w_query: bfloat16 [512, 512], replicated, may hold values from -0.3 to 0.3
- w_key: bfloat16 [512, 512], replicated, may hold values from -0.3 to 0.3
- w_value: bfloat16 [512, 512], replicated, may hold values from -0.25 to 0.25
- neighbour: int32 [65536, 16], P(('lon', 'lat')), may hold values from 0 to 767, as said below
- slot_mask: int32 [65536, 16], P(('lon', 'lat')), may hold values 0 or 1
- send_rows: int32 [1024, 128], P(('lon', 'lat')), may hold values from 0 to 255
Outputs:
- features_grad: bfloat16 [65536, 512], P(('lon', 'lat'))
- weight_grads: float32 [1536, 512], P(('lon', 'lat'))
The draws below stay inside these ranges and needn't reach their ends.
Inputs may be any that keep to these rules, and one draw needn't show every extreme that they name: `neighbour`: the 16 slots of a node name 16 different rows of its sector's table.
All inputs are finite; a program needn't handle non-finite values. No bound on the sum of `slot_mask` on one device may be relied on, other than what follows from the above.
Results may differ from the reference program's by a relative error of at most 0.02.
Values may be sent and summed in bfloat16 or wider, within the bound.
A program may use at most 128 MiB of HBM per device.

```python
import math
import jax
import jax.numpy as jnp
from jax import lax

D = 512
HEADS = 4
SLOTS = 16
NDEV = 256
HSEND = 128
NODES = 65536
N_LON = 32
N_LAT = 8
DEVICES = 256


def draw_features(key, part):
    key = jax.random.fold_in(key, 3)
    noise_key = jax.random.fold_in(key, 0)
    values = jnp.clip(jax.random.normal(noise_key, (NODES, D), jnp.float32), -6.0, 6.0)
    return values.astype(jnp.bfloat16)


def draw_w_query(key, part):
    key = jax.random.fold_in(key, 5)
    values = jax.random.truncated_normal(key, -4.0, 4.0, (D, D), jnp.float32) / math.sqrt(D)
    return values.astype(jnp.bfloat16)


def draw_w_key(key, part):
    key = jax.random.fold_in(key, 9)
    values = jax.random.truncated_normal(key, -4.0, 4.0, (D, D), jnp.float32) / math.sqrt(D)
    return values.astype(jnp.bfloat16)


def draw_neighbour(key, part):
    key = jax.random.fold_in(key, 7)
    first_key, spacing_key, priority_key = jax.random.split(key, 3)
    table_rows = NDEV + 4 * HSEND
    first_row = jax.random.randint(first_key, (NODES, 1), 0, table_rows, dtype=jnp.int32)
    spacing = jax.random.randint(spacing_key, (NODES, SLOTS), 1, table_rows // SLOTS + 1, dtype=jnp.int32)
    spread_rows = (first_row + jnp.cumsum(spacing, axis=1)) % table_rows
    priority = jax.random.randint(priority_key, (NODES, SLOTS), 0, 1 << 20, dtype=jnp.int32) * SLOTS
    priority = priority + jnp.arange(SLOTS, dtype=jnp.int32)[None, :]
    shuffle_order = jnp.argsort(priority, axis=1)
    return jnp.take_along_axis(spread_rows, shuffle_order, axis=1).astype(jnp.int32)


def with_ends(values, key, least, high):
    longest = values.shape.index(max(values.shape))
    spots = []
    for shift in (0, 1):
        where = [jax.random.randint(jax.random.fold_in(key, axis), (), 0, length) for axis, length in enumerate(values.shape)]
        where[longest] = (where[longest] + shift) % values.shape[longest]
        spots.append(tuple(where))
    return values.at[spots[0]].set(least).at[spots[1]].set(high)


def level_of(own_key, shape, shards, smallest, high):
    level, own = 1.0, jax.random.fold_in(own_key, 6)
    for axis_at, blocks in shards:
        heights = jnp.exp(jax.random.uniform(jax.random.fold_in(own, axis_at), (blocks,), jnp.float32, smallest / len(shards), high / len(shards)))
        level = level * jnp.repeat(heights, shape[axis_at] // blocks).reshape([-1 if axis == axis_at else 1 for axis in range(len(shape))])
    return level


def centred(rng, dims, spread, reach, pieces=(), held_as=jnp.bfloat16):
    drawn = spread * jax.random.normal(rng, dims, jnp.float32)
    if pieces:
        drawn = drawn * level_of(rng, dims, pieces, -0.22, 0.18)
    return jnp.clip(drawn, -reach, reach).astype(held_as)


def setup_inputs(seed: int = 0) -> dict:
    seeds = jax.random.split(jax.random.key(seed), 9)
    features = draw_features(jax.random.fold_in(seeds[8], 71), 0)
    cotangent = centred(seeds[1], (NODES, D), 1.0, 6.0, ((0, 256),))
    w_query = draw_w_query(jax.random.fold_in(seeds[8], 71), 0)
    w_key = draw_w_key(jax.random.fold_in(seeds[8], 71), 0)
    w_value = centred(seeds[4], (D, D), D ** -0.5, 0.25)
    neighbour = draw_neighbour(jax.random.fold_in(seeds[8], 71), 0)
    slot_mask = with_ends((jax.random.randint(seeds[6], (NODES, SLOTS), 0, 4) < 3).astype(jnp.int32), jax.random.fold_in(seeds[6], 1), 0, 1)
    send_rows = with_ends(jax.random.randint(seeds[7], (4 * DEVICES, HSEND), 0, NDEV), jax.random.fold_in(seeds[7], 1), 0, NDEV - 1).astype(jnp.int32)
    return dict(features=features, cotangent=cotangent, w_query=w_query, w_key=w_key, w_value=w_value, neighbour=neighbour, slot_mask=slot_mask, send_rows=send_rows)


def source_rows(neighbour, send_rows):
    device_ids = jnp.arange(DEVICES, dtype=jnp.int32)
    lon_index = device_ids // N_LAT
    lat_index = device_ids % N_LAT
    send_lists = send_rows.reshape(DEVICES, 4, HSEND)
    lon_lower = ((lon_index - 1) % N_LON) * N_LAT + lat_index
    lon_upper = ((lon_index + 1) % N_LON) * N_LAT + lat_index
    lat_lower = lon_index * N_LAT + jnp.maximum(lat_index - 1, 0)
    lat_upper = lon_index * N_LAT + jnp.minimum(lat_index + 1, N_LAT - 1)
    missing = jnp.full((DEVICES, HSEND), -1, jnp.int32)
    halo_blocks = [
        send_lists[lon_lower, 1] + (lon_lower * NDEV)[:, None],
        send_lists[lon_upper, 0] + (lon_upper * NDEV)[:, None],
        jnp.where((lat_index > 0)[:, None], send_lists[lat_lower, 3] + (lat_lower * NDEV)[:, None], missing),
        jnp.where((lat_index < N_LAT - 1)[:, None], send_lists[lat_upper, 2] + (lat_upper * NDEV)[:, None], missing),
    ]
    own_rows = (device_ids * NDEV)[:, None] + jnp.arange(NDEV, dtype=jnp.int32)[None, :]
    lookup = jnp.concatenate([own_rows] + halo_blocks, axis=1).astype(jnp.int32)
    local_index = neighbour.reshape(DEVICES, NDEV * SLOTS).astype(jnp.int32)
    return jnp.take_along_axis(lookup, local_index, axis=1).reshape(NODES, SLOTS)


def attend_back(queries, grad_out, gathered, usable):
    row_count = queries.shape[0]
    head_size = D // HEADS
    score_scale = head_size ** -0.5
    query_heads = queries.astype(jnp.float32).reshape(row_count, HEADS, head_size)
    grad_heads = grad_out.astype(jnp.float32).reshape(row_count, HEADS, head_size)
    key_heads = gathered[:, :, :D].astype(jnp.float32).reshape(row_count, SLOTS, HEADS, head_size)
    value_heads = gathered[:, :, D:].astype(jnp.float32).reshape(row_count, SLOTS, HEADS, head_size)
    scores = jnp.einsum("rhd,rshd->rsh", query_heads, key_heads) * score_scale
    allowed = usable[:, :, None] > 0
    masked = jnp.where(allowed, scores, -1e30)
    largest = jnp.max(masked, axis=1, keepdims=True)
    expvals = jnp.where(allowed, jnp.exp(masked - largest), 0.0)
    probability = expvals / jnp.sum(expvals, axis=1, keepdims=True)
    rounded = probability.astype(jnp.bfloat16)
    grad_prob = jnp.einsum("rhd,rshd->rsh", grad_heads, value_heads)
    inner_sum = jnp.sum(probability * grad_prob, axis=1, keepdims=True)
    grad_score = (probability * (grad_prob - inner_sum) * score_scale).astype(jnp.bfloat16)
    score_wide = grad_score.astype(jnp.float32)
    grad_query = jnp.einsum("rsh,rshd->rhd", score_wide, key_heads).reshape(row_count, D).astype(jnp.bfloat16)
    grad_key = score_wide[..., None] * query_heads[:, None]
    grad_value = rounded.astype(jnp.float32)[..., None] * grad_heads[:, None]
    contrib = jnp.concatenate([grad_key.reshape(row_count, SLOTS, D), grad_value.reshape(row_count, SLOTS, D)], axis=2)
    return grad_query, contrib


def reference(features, cotangent, w_query, w_key, w_value, neighbour, slot_mask, send_rows):
    source = source_rows(neighbour, send_rows)
    source = jnp.where(source >= 0, source, NODES).astype(jnp.int32)
    first_slot = (jnp.arange(SLOTS) == 0).astype(jnp.int32)
    usable = jnp.maximum(slot_mask, first_slot[None, :])
    queries = jnp.dot(features, w_query, preferred_element_type=jnp.float32).astype(jnp.bfloat16)
    key_rows = jnp.dot(features, w_key, preferred_element_type=jnp.float32).astype(jnp.bfloat16)
    value_rows = jnp.dot(features, w_value, preferred_element_type=jnp.float32).astype(jnp.bfloat16)
    padded = jnp.concatenate([key_rows, value_rows], axis=1)
    padded = jnp.concatenate([padded, jnp.zeros((1, 2 * D), padded.dtype)], axis=0)

    def one_device(totals, inputs):
        query_block, grad_block, index_block, mask_block = inputs
        grad_query, contrib = attend_back(query_block, grad_block, padded[index_block], mask_block)
        return totals.at[index_block].add(contrib), grad_query

    totals = jnp.zeros((NODES + 1, 2 * D), jnp.float32)
    totals, grad_query = lax.scan(one_device, totals, (
        queries.reshape(DEVICES, NDEV, D),
        cotangent.reshape(DEVICES, NDEV, D),
        source.reshape(DEVICES, NDEV, SLOTS),
        usable.reshape(DEVICES, NDEV, SLOTS)))
    stacked = jnp.concatenate([grad_query.reshape(NODES, D), totals[:NODES].astype(jnp.bfloat16)], axis=1)
    weights = jnp.concatenate([w_query, w_key, w_value], axis=1)
    features_grad = lax.dot_general(stacked, weights, (((1,), (1,)), ((), ())), preferred_element_type=jnp.float32).astype(jnp.bfloat16)
    weight_grads = lax.dot_general(stacked, features, (((0,), (0,)), ((), ())), preferred_element_type=jnp.float32)
    return features_grad, weight_grads
```

```python
import jax
import jax.numpy as jnp
import numpy as np
from jax import lax
from jax.experimental import pallas as pl
from jax.experimental.pallas import tpu as pltpu
from jax.sharding import PartitionSpec as P

MESH = pl.DeviceIdType.MESH
F32, BF16, I32 = jnp.float32, jnp.bfloat16, jnp.int32
D, HEADS, SLOTS, ROWS, HALO = 512, 4, 16, 256, 128
HEAD = D // HEADS
TABLE = ROWS + 4 * HALO
SCALE = HEAD ** -0.5
NN = (((1,), (0,)), ((), ()))
NT = (((1,), (1,)), ((), ()))
TN = (((0,), (0,)), ((), ()))
VMEM = pltpu.VMEM
DMA = pltpu.SemaphoreType.DMA


def dot(a, b, dims=NN):
    return lax.dot_general(a, b, dims, preferred_element_type=F32)


def kernel(
    feat, cot, w_query, w_key, w_value, nbr, msk, snd, perm,
    fg_out, dw_out,
    ftab, cot_v, w_v, nbr_v, msk_v, snd_v, perm_v,
    picked, q_v, k_v, v_v, bias, s_v, dp_v, p_v, ds_v, gq_v, gk_v, gv_v, dw_v,
    part, crecv, acc1, precv, acc2, zsend, zrecv, fg_own, fgh_s, fgh_r,
    in_sem, hs_sem, hr_sem, cs_sem, cr_sem, ps_sem, pr_sem, zs_sem, zr_sem, rs_sem, rr_sem,
):
    lon, lat = lax.axis_index("lon"), lax.axis_index("lat")
    z, yh, core = lon // 4, (lon // 2) % 2, lon % 2
    plane = yh * 8 + lat
    partner = (lon + 1 - 2 * core, lat)
    plane_peers = []
    for d in range(1, 16):
        other = (plane + d) % 16
        plane_peers.append((z * 4 + (other // 8) * 2 + core, other % 8))
    z_peers = [(((z + d) % 8) * 4 + yh * 2 + core, lat) for d in range(1, 8)]
    lon_lo, lon_hi = (lon + 31) % 32, (lon + 1) % 32
    lat_lo, lat_hi = (lat + 7) % 8, (lat + 1) % 8
    far = ((lon + 31 + 2 * core) % 32, lat)
    sides = [(lon_lo, lat), (lon_hi, lat), (lon, lat_lo), (lon, lat_hi)]
    lands = (1, 0, 3, 2)

    barrier = pltpu.get_barrier_semaphore()
    peers = [partner, far] + plane_peers + z_peers
    for peer in peers:
        pl.semaphore_signal(barrier, inc=1, device_id=peer, device_id_type=MESH)

    loads = []
    for i, (src, dst) in enumerate(
        [
            (snd, snd_v), (feat, ftab.at[pl.ds(0, ROWS)]), (w_query, w_v.at[0]), (w_key, w_v.at[1]),
            (w_value, w_v.at[2]), (nbr, nbr_v), (msk, msk_v), (cot, cot_v), (perm, perm_v),
        ]
    ):
        load = pltpu.make_async_copy(src, dst, in_sem.at[i])
        load.start()
        loads.append(load)

    loads[0].wait()
    loads[1].wait()
    row_ids = lax.broadcasted_iota(I32, (ROWS, HALO), 0)
    for l in range(4):
        chosen = (row_ids == snd_v[l : l + 1, :]).astype(F32).astype(BF16)
        picked[:, l * HALO : (l + 1) * HALO] = chosen
        fgh_s[l] = dot(chosen, ftab[0:ROWS, :], TN).astype(BF16)
    pl.semaphore_wait(barrier, len(peers))
    halo = []
    for l in range(4):
        copy = pltpu.make_async_remote_copy(
            src_ref=fgh_s.at[l],
            dst_ref=ftab.at[pl.ds(ROWS + lands[l] * HALO, HALO)],
            send_sem=hs_sem.at[l],
            recv_sem=hr_sem.at[lands[l]],
            device_id=sides[l],
            device_id_type=MESH,
        )
        copy.start()
        halo.append(copy)

    loads[2].wait()
    loads[3].wait()
    loads[4].wait()
    own = ftab[0:ROWS, :]
    q_v[...] = dot(own, w_v[0]).astype(BF16)
    k_v[0:ROWS, :] = dot(own, w_v[1]).astype(BF16)
    v_v[0:ROWS, :] = dot(own, w_v[2]).astype(BF16)
    loads[5].wait()
    loads[6].wait()
    slot_ids = lax.broadcasted_iota(I32, (ROWS, SLOTS), 1)
    wanted = jnp.where((msk_v[...] > 0) | (slot_ids == 0), nbr_v[...], -1)
    wanted = jnp.transpose(wanted)
    tile = 32
    for t in range(TABLE // tile):
        ids = lax.broadcasted_iota(I32, (tile, ROWS), 0) + t * tile
        b = jnp.full((tile, ROWS), -1e30, F32)
        for j in range(SLOTS):
            b = jnp.where(ids == wanted[j : j + 1, :], 0.0, b)
        bias[t * tile : (t + 1) * tile, :] = b
    loads[7].wait()
    loads[8].wait()

    def products(lo, hi):
        for h in range(HEADS):
            cols = slice(h * HEAD, (h + 1) * HEAD)
            s_v[h, lo:hi, :] = dot(k_v[lo:hi, cols], q_v[:, cols], NT)
            dp_v[h, lo:hi, :] = dot(v_v[lo:hi, cols], cot_v[:, cols], NT)

    products(0, ROWS)

    for b in range(4):
        halo[b].wait_recv()

    @pl.when(lat == 0)
    def _():
        ftab[ROWS + 2 * HALO : ROWS + 3 * HALO, :] = jnp.zeros((HALO, D), BF16)

    @pl.when(lat == 7)
    def _():
        ftab[ROWS + 3 * HALO : ROWS + 4 * HALO, :] = jnp.zeros((HALO, D), BF16)

    others = ftab[ROWS:TABLE, :]
    k_v[ROWS:TABLE, :] = dot(others, w_v[1]).astype(BF16)
    v_v[ROWS:TABLE, :] = dot(others, w_v[2]).astype(BF16)
    products(ROWS, TABLE)

    step = 64
    for h in range(HEADS):
        top = jnp.full((8, ROWS), -3e38, F32)
        for t in range(0, TABLE, step):
            s = s_v[h, t : t + step, :] + bias[t : t + step, :]
            s_v[h, t : t + step, :] = s
            top = jnp.maximum(top, jnp.max(s.reshape(step // 8, 8, ROWS), axis=0))
        top = jnp.max(top, axis=0, keepdims=True)
        total = jnp.zeros((8, ROWS), F32)
        inner = jnp.zeros((8, ROWS), F32)
        for t in range(0, TABLE, step):
            e = jnp.exp((s_v[h, t : t + step, :] - top) * SCALE)
            s_v[h, t : t + step, :] = e
            total += jnp.sum(e.reshape(step // 8, 8, ROWS), axis=0)
            inner += jnp.sum((e * dp_v[h, t : t + step, :]).reshape(step // 8, 8, ROWS), axis=0)
        inverse = 1.0 / jnp.sum(total, axis=0, keepdims=True)
        inner = jnp.sum(inner, axis=0, keepdims=True) * inverse
        for t in range(0, TABLE, step):
            p = s_v[h, t : t + step, :] * inverse
            p_v[h, t : t + step, :] = p.astype(BF16)
            ds_v[h, t : t + step, :] = (p * (dp_v[h, t : t + step, :] - inner) * SCALE).astype(BF16)
        cols = slice(h * HEAD, (h + 1) * HEAD)
        gv_v[:, cols] = dot(p_v[h], cot_v[:, cols]).astype(BF16)
        gk_v[:, cols] = dot(ds_v[h], q_v[:, cols]).astype(BF16)
        gq_v[:, cols] = dot(ds_v[h], k_v[:, cols], TN).astype(BF16)

    dw_v[0:D, :] = dot(gq_v[...], own, TN).astype(BF16)
    dw_v[D : 2 * D, :] = dot(gk_v[...], ftab[...], TN).astype(BF16)
    dw_v[2 * D : 3 * D, :] = dot(gv_v[...], ftab[...], TN).astype(BF16)

    core_copies = []
    for c in range(2):
        for half in range(2):
            for y in range(2):
                rows = jnp.concatenate(
                    [dw_v[pl.ds((c * 4 + zz) * 192 + y * 96 + half * 48, 48), :] for zz in range(4)], axis=0
                )
                sorted_rows = dot(perm_v[...], rows)
                for k in range(8):
                    block = sorted_rows[k * 24 : (k + 1) * 24, :]
                    block = jnp.concatenate([block[:, 0:256], block[:, 256:512]], axis=0)
                    part[c, half, y * 8 + k] = block.astype(BF16)
        copy = pltpu.make_async_remote_copy(
            src_ref=part.at[c, 1 - core],
            dst_ref=crecv.at[c],
            send_sem=cs_sem.at[c],
            recv_sem=cr_sem.at[c],
            device_id=partner,
            device_id_type=MESH,
        )
        copy.start()
        core_copies.append(copy)

    plane_copies = []
    for c in range(2):
        core_copies[c].wait_recv()
        for k in range(16):
            acc1[c, k] = (part[c, core, k].astype(F32) + crecv[c, k].astype(F32)).astype(BF16)
        for d in range(1, 16):
            copy = pltpu.make_async_remote_copy(
                src_ref=acc1.at[c, (plane + d) % 16],
                dst_ref=precv.at[c, d - 1],
                send_sem=ps_sem.at[c, d - 1],
                recv_sem=pr_sem.at[c, d - 1],
                device_id=plane_peers[d - 1],
                device_id_type=MESH,
            )
            copy.start()
            plane_copies.append(copy)

    for copy in halo:
        copy.wait_send()
    back = []
    for b in range(4):
        rows = slice(ROWS + b * HALO, ROWS + (b + 1) * HALO)
        fgh_s[b] = (dot(gk_v[rows, :], w_v[1], NT) + dot(gv_v[rows, :], w_v[2], NT)).astype(BF16)
        copy = pltpu.make_async_remote_copy(
            src_ref=fgh_s.at[b],
            dst_ref=fgh_r.at[pl.ds(lands[b] * HALO, HALO)],
            send_sem=rs_sem.at[b],
            recv_sem=rr_sem.at[lands[b]],
            device_id=sides[b],
            device_id_type=MESH,
        )
        copy.start()
        back.append(copy)
    fg_own[...] = (
        dot(gq_v[...], w_v[0], NT) + dot(gk_v[0:ROWS, :], w_v[1], NT) + dot(gv_v[0:ROWS, :], w_v[2], NT)
    )

    z_copies = []
    for c in range(2):
        total = acc1[c, plane].astype(F32)
        for d in range(1, 16):
            plane_copies[c * 15 + d - 1].wait_recv()
            total += precv[c, d - 1].astype(F32)
        acc2[0:24, :] = jnp.concatenate([total[0:24, :], total[24:48, :]], axis=1)
        acc2[24:32, :] = jnp.zeros((8, D), F32)
        for zz in range(4):
            zsend[c * 4 + zz] = acc2[zz * 6 : zz * 6 + 8, :]
    for d in range(1, 8):
        copy = pltpu.make_async_remote_copy(
            src_ref=zsend.at[(z + d) % 8],
            dst_ref=zrecv.at[d - 1],
            send_sem=zs_sem.at[d - 1],
            recv_sem=zr_sem.at[d - 1],
            device_id=z_peers[d - 1],
            device_id_type=MESH,
        )
        copy.start()
        z_copies.append(copy)

    for b in range(4):
        back[b].wait_recv()

    @pl.when(lat == 0)
    def _():
        fgh_r[2 * HALO : 3 * HALO, :] = jnp.zeros((HALO, D), BF16)

    @pl.when(lat == 7)
    def _():
        fgh_r[3 * HALO : 4 * HALO, :] = jnp.zeros((HALO, D), BF16)

    fg_out[...] = (fg_own[...] + dot(picked[...], fgh_r[...])).astype(BF16)

    for copy in back + core_copies + plane_copies:
        copy.wait_send()
    total = zsend[z]
    for d in range(1, 8):
        z_copies[d - 1].wait_recv()
        total += zrecv[d - 1]
    dw_out[...] = total[0:6, :]
    for copy in z_copies:
        copy.wait_send()


def sorting():
    source = np.arange(192).reshape(4, 8, 6).transpose(1, 0, 2).reshape(-1)
    return (source[:, None] == np.arange(192)[None, :]).astype(np.float32)


def shards(features, cotangent, w_query, w_key, w_value, neighbour, slot_mask, send_rows):
    whole = pl.BlockSpec(memory_space=VMEM)
    return pl.pallas_call(
        kernel,
        out_shape=(jax.ShapeDtypeStruct((ROWS, D), BF16), jax.ShapeDtypeStruct((6, D), F32)),
        in_specs=[pl.BlockSpec(memory_space=pl.ANY)] * 9,
        out_specs=(whole, whole),
        scratch_shapes=[
            VMEM((TABLE, D), BF16), VMEM((ROWS, D), BF16), VMEM((3, D, D), BF16), VMEM((ROWS, SLOTS), I32),
            VMEM((ROWS, SLOTS), I32), VMEM((4, HALO), I32), VMEM((192, 192), BF16),
            VMEM((ROWS, 4 * HALO), BF16), VMEM((ROWS, D), BF16), VMEM((TABLE, D), BF16), VMEM((TABLE, D), BF16),
            VMEM((TABLE, ROWS), F32), VMEM((HEADS, TABLE, ROWS), F32), VMEM((HEADS, TABLE, ROWS), F32),
            VMEM((HEADS, TABLE, ROWS), BF16), VMEM((HEADS, TABLE, ROWS), BF16),
            VMEM((ROWS, D), BF16), VMEM((TABLE, D), BF16), VMEM((TABLE, D), BF16), VMEM((3 * D, D), BF16),
            VMEM((2, 2, 16, 48, 256), BF16), VMEM((2, 16, 48, 256), BF16), VMEM((2, 16, 48, 256), BF16),
            VMEM((2, 15, 48, 256), BF16), VMEM((32, D), F32), VMEM((8, 8, D), F32), VMEM((7, 8, D), F32),
            VMEM((ROWS, D), F32), VMEM((4, HALO, D), BF16), VMEM((4 * HALO, D), BF16),
            DMA((9,)), DMA((4,)), DMA((4,)), DMA((2,)), DMA((2,)), DMA((2, 15)), DMA((2, 15)),
            DMA((7,)), DMA((7,)), DMA((4,)), DMA((4,)),
        ],
        compiler_params=pltpu.CompilerParams(
            collective_id=0, has_side_effects=True, vmem_limit_bytes=48 * 1024 * 1024
        ),
        name="mesh_attention_backward",
    )(
        features, cotangent, w_query, w_key, w_value, neighbour, slot_mask, send_rows,
        jnp.asarray(sorting(), BF16),
    )


def solution(mesh):
    rows = P(("lon", "lat"), None)
    return jax.shard_map(
        shards,
        mesh=mesh,
        in_specs=(rows, rows, P(), P(), P(), rows, rows, rows),
        out_specs=(rows, rows),
        check_vma=False,
    )
```

```python
import jax
import jax.numpy as jnp
import numpy as np
from jax import lax
from jax.experimental import pallas as pl
from jax.experimental.pallas import tpu as pltpu
from jax.sharding import PartitionSpec as P

MESH = pl.DeviceIdType.MESH
F32, BF16, I32 = jnp.float32, jnp.bfloat16, jnp.int32
D, HEADS, SLOTS, ROWS, HALO = 512, 4, 16, 256, 128
HEAD = D // HEADS
TABLE = ROWS + 4 * HALO
SCALE = HEAD ** -0.5
NN = (((1,), (0,)), ((), ()))
NT = (((1,), (1,)), ((), ()))
TN = (((0,), (0,)), ((), ()))
VMEM = pltpu.VMEM
OFFSETS = sorted(
    ((dy, dx) for dy in range(4) for dx in range(4) if dy or dx),
    key=lambda at: -(min(at[0], 4 - at[0]) + min(at[1], 4 - at[1])),
)
DMA = pltpu.SemaphoreType.DMA


def dot(a, b, dims=NN):
    return lax.dot_general(a, b, dims, preferred_element_type=F32)


def kernel(
    feat, cot, w_query, w_key, w_value, nbr, msk, snd, perm,
    fg_out, dw_out,
    ftab, cot_v, w_v, nbr_v, msk_v, snd_v, perm_v,
    picked, q_v, k_v, v_v, bias, s_v, dp_v, p_v, ds_v, gq_v, gk_v, gv_v, dw_v,
    part, crecv, acc1, precv, acc2, zsend, zrecv, fg_own, fgh_s, fgh_r,
    in_sem, hs_sem, hr_sem, cs_sem, cr_sem, ps_sem, pr_sem, zs_sem, zr_sem, rs_sem, rr_sem,
):
    lon, lat = lax.axis_index("lon"), lax.axis_index("lat")
    z, core = lon // 4, lon % 2
    y, x = ((lon // 2) % 2) * 2 + lat // 4, lat % 4
    plane = y * 4 + x
    partner = (lon + 1 - 2 * core, lat)
    planes, plane_peers = [], []
    for dy, dx in OFFSETS:
        other_y, other_x = (y + dy) % 4, (x + dx) % 4
        planes.append(other_y * 4 + other_x)
        plane_peers.append((z * 4 + (other_y // 2) * 2 + core, (other_y % 2) * 4 + other_x))
    z_peers = [(other * 4 + lon % 4, lat) for other in range(8)]
    lat_lo, lat_hi = (lat + 7) % 8, (lat + 1) % 8
    far = ((lon + 31 + 2 * core) % 32, lat)
    sides = [(core, 1 - core, far), (2, 3, (lon, lat_lo)), (3, 2, (lon, lat_hi)), (1 - core, core, partner)]

    def load(i, src, dst):
        copy = pltpu.make_async_copy(src, dst, in_sem.at[i])
        copy.start()
        return copy

    rows_in = [load(0, snd, snd_v), load(1, feat, ftab.at[pl.ds(0, ROWS)])]
    barrier = pltpu.get_barrier_semaphore()
    peers = [far, partner] + plane_peers + [(((z + d) % 8) * 4 + lon % 4, lat) for d in (4, 3, 5, 2, 6, 1, 7)]
    for peer in peers:
        pl.semaphore_signal(barrier, inc=1, device_id=peer, device_id_type=MESH)

    for copy in rows_in:
        copy.wait()
    weights_in = [load(2, w_query, w_v.at[0]), load(3, w_key, w_v.at[1]), load(4, w_value, w_v.at[2])]
    slots_in = [load(5, nbr, nbr_v), load(6, msk, msk_v)]
    rest_in = [load(7, cot, cot_v), load(8, perm, perm_v)]
    row_ids = lax.broadcasted_iota(I32, (ROWS, HALO), 0)
    for l in range(4):
        chosen = (row_ids == snd_v[l : l + 1, :]).astype(F32).astype(BF16)
        picked[:, l * HALO : (l + 1) * HALO] = chosen
        fgh_s[l] = dot(chosen, ftab[0:ROWS, :], TN).astype(BF16)
    pl.semaphore_wait(barrier, len(peers))
    halo = []
    for i, (l, block, device) in enumerate(sides):
        copy = pltpu.make_async_remote_copy(
            src_ref=fgh_s.at[l],
            dst_ref=ftab.at[pl.ds(ROWS + block * HALO, HALO)],
            send_sem=hs_sem.at[i],
            recv_sem=hr_sem.at[i],
            device_id=device,
            device_id_type=MESH,
        )
        copy.start()
        halo.append(copy)

    for copy in weights_in:
        copy.wait()
    own = ftab[0:ROWS, :]
    q_v[...] = dot(own, w_v[0]).astype(BF16)
    k_v[0:ROWS, :] = dot(own, w_v[1]).astype(BF16)
    v_v[0:ROWS, :] = dot(own, w_v[2]).astype(BF16)
    for copy in slots_in:
        copy.wait()
    slot_ids = lax.broadcasted_iota(I32, (SLOTS, ROWS), 0)
    wanted = jnp.where((msk_v[...] > 0) | (slot_ids == 0), nbr_v[...], -1)
    tile = 32
    for t in range(TABLE // tile):
        ids = lax.broadcasted_iota(I32, (tile, ROWS), 0) + t * tile
        b = jnp.full((tile, ROWS), -1e30, F32)
        for j in range(SLOTS):
            b = jnp.where(ids == wanted[j : j + 1, :], 0.0, b)
        bias[t * tile : (t + 1) * tile, :] = b
    for copy in rest_in:
        copy.wait()

    step = 64
    tops = [jnp.full((8, ROWS), -3e38, F32) for _ in range(HEADS)]

    def products(lo, hi):
        for h in range(HEADS):
            cols = slice(h * HEAD, (h + 1) * HEAD)
            s_v[h, lo:hi, :] = dot(k_v[lo:hi, cols], q_v[:, cols], NT)
            dp_v[h, lo:hi, :] = dot(v_v[lo:hi, cols], cot_v[:, cols], NT)
            for t in range(lo, hi, step):
                s = s_v[h, t : t + step, :] + bias[t : t + step, :]
                s_v[h, t : t + step, :] = s
                tops[h] = jnp.maximum(tops[h], jnp.max(s.reshape(step // 8, 8, ROWS), axis=0))

    products(0, ROWS)

    for copy in halo:
        copy.wait_recv()

    @pl.when(lat == 0)
    def _():
        ftab[ROWS + 2 * HALO : ROWS + 3 * HALO, :] = jnp.zeros((HALO, D), BF16)

    @pl.when(lat == 7)
    def _():
        ftab[ROWS + 3 * HALO : ROWS + 4 * HALO, :] = jnp.zeros((HALO, D), BF16)

    others = ftab[ROWS:TABLE, :]
    k_v[ROWS:TABLE, :] = dot(others, w_v[1]).astype(BF16)
    v_v[ROWS:TABLE, :] = dot(others, w_v[2]).astype(BF16)
    products(ROWS, TABLE)

    for h in range(HEADS):
        cols = slice(h * HEAD, (h + 1) * HEAD)
        top = jnp.max(tops[h], axis=0, keepdims=True)
        total = jnp.zeros((8, ROWS), F32)
        inner = jnp.zeros((8, ROWS), F32)
        for t in range(0, TABLE, step):
            e = jnp.exp((s_v[h, t : t + step, :] - top) * SCALE)
            s_v[h, t : t + step, :] = e
            total += jnp.sum(e.reshape(step // 8, 8, ROWS), axis=0)
            inner += jnp.sum((e * dp_v[h, t : t + step, :]).reshape(step // 8, 8, ROWS), axis=0)
        inverse = 1.0 / jnp.sum(total, axis=0, keepdims=True)
        inner = jnp.sum(inner, axis=0, keepdims=True) * inverse
        for t in range(0, TABLE, step):
            p = s_v[h, t : t + step, :] * inverse
            p_v[h, t : t + step, :] = p.astype(BF16)
            ds_v[h, t : t + step, :] = (p * (dp_v[h, t : t + step, :] - inner) * SCALE).astype(BF16)
        gq_v[:, cols] = dot(ds_v[h], k_v[:, cols], TN).astype(BF16)
        if h < 2:
            gk_v[:, cols] = dot(ds_v[h], q_v[:, cols]).astype(BF16)

    def to_partner(c):
        for half in range(2):
            for y_hi in range(2):
                rows = jnp.concatenate(
                    [dw_v[pl.ds((c * 4 + zz) * 192 + y_hi * 96 + half * 48, 48), :] for zz in range(4)], axis=0
                )
                sorted_rows = dot(perm_v[...], rows)
                for k in range(8):
                    block = sorted_rows[k * 24 : (k + 1) * 24, :]
                    block = jnp.concatenate([block[:, 0:256], block[:, 256:512]], axis=0)
                    part[c, half, y_hi * 8 + k] = block.astype(BF16)
        copy = pltpu.make_async_remote_copy(
            src_ref=part.at[c, 1 - core],
            dst_ref=crecv.at[c],
            send_sem=cs_sem.at[c],
            recv_sem=cr_sem.at[c],
            device_id=partner,
            device_id_type=MESH,
        )
        copy.start()
        return copy

    def to_plane(c, from_partner):
        from_partner.wait_recv()
        copies = []
        for i, other in enumerate(planes):
            acc1[c, other] = (part[c, core, other].astype(F32) + crecv[c, other].astype(F32)).astype(BF16)
            copy = pltpu.make_async_remote_copy(
                src_ref=acc1.at[c, other],
                dst_ref=precv.at[c, i],
                send_sem=ps_sem.at[c, i],
                recv_sem=pr_sem.at[c, i],
                device_id=plane_peers[i],
                device_id_type=MESH,
            )
            copy.start()
            copies.append(copy)
        return copies

    def to_z(c, from_plane):
        total = part[c, core, plane].astype(F32) + crecv[c, plane].astype(F32)
        for i, copy in enumerate(from_plane):
            copy.wait_recv()
            total += precv[c, i].astype(F32)
        acc2[c, 0:24, :] = jnp.concatenate([total[0:24, :], total[24:48, :]], axis=1)
        acc2[c, 24:32, :] = jnp.zeros((8, D), F32)
        copies = []
        for zz in range(4):
            other = c * 4 + zz
            rows = acc2[c, zz * 6 : zz * 6 + 8, :]
            zsend[other] = jnp.concatenate([rows[:, 0:256], rows[:, 256:512]], axis=0).astype(BF16)
            copy = pltpu.make_async_remote_copy(
                src_ref=zsend.at[other],
                dst_ref=zrecv.at[z],
                send_sem=zs_sem.at[other],
                recv_sem=zr_sem.at[z],
                device_id=z_peers[other],
                device_id_type=MESH,
            )
            pl.when(z != other)(copy.start)
        return copies

    dw_v[0:D, :] = dot(gq_v[...], own, TN).astype(BF16)
    dw_v[D : D + 256, :] = dot(gk_v[:, 0:256], ftab[...], TN).astype(BF16)
    core_a = to_partner(0)
    for h in range(HEADS):
        cols = slice(h * HEAD, (h + 1) * HEAD)
        gv_v[:, cols] = dot(p_v[h], cot_v[:, cols]).astype(BF16)
        if h >= 2:
            gk_v[:, cols] = dot(ds_v[h], q_v[:, cols]).astype(BF16)
    dw_v[D + 256 : 2 * D, :] = dot(gk_v[:, 256:512], ftab[...], TN).astype(BF16)
    dw_v[2 * D : 3 * D, :] = dot(gv_v[...], ftab[...], TN).astype(BF16)
    plane_a = to_plane(0, core_a)
    core_b = to_partner(1)
    fg_own[...] = (
        dot(gq_v[...], w_v[0], NT) + dot(gk_v[0:ROWS, :], w_v[1], NT) + dot(gv_v[0:ROWS, :], w_v[2], NT)
    )
    plane_b = to_plane(1, core_b)

    for copy in halo:
        copy.wait_send()
    for b in range(4):
        rows = slice(ROWS + b * HALO, ROWS + (b + 1) * HALO)
        fgh_s[b] = (dot(gk_v[rows, :], w_v[1], NT) + dot(gv_v[rows, :], w_v[2], NT)).astype(BF16)
    to_z(0, plane_a)
    back = []
    for i, (b, block, device) in enumerate(sides):
        copy = pltpu.make_async_remote_copy(
            src_ref=fgh_s.at[b],
            dst_ref=fgh_r.at[pl.ds(block * HALO, HALO)],
            send_sem=rs_sem.at[i],
            recv_sem=rr_sem.at[i],
            device_id=device,
            device_id_type=MESH,
        )
        copy.start()
        back.append(copy)
    to_z(1, plane_b)

    for copy in back:
        copy.wait_recv()

    @pl.when(lat == 0)
    def _():
        fgh_r[2 * HALO : 3 * HALO, :] = jnp.zeros((HALO, D), BF16)

    @pl.when(lat == 7)
    def _():
        fgh_r[3 * HALO : 4 * HALO, :] = jnp.zeros((HALO, D), BF16)

    fg_out[...] = (fg_own[...] + dot(picked[...], fgh_r[...])).astype(BF16)

    for copy in back + [core_a, core_b] + plane_a + plane_b:
        copy.wait_send()
    zrecv[z] = zsend[z]
    for other in range(8):
        copy = pltpu.make_async_remote_copy(
            src_ref=zsend.at[other],
            dst_ref=zrecv.at[other],
            send_sem=zs_sem.at[other],
            recv_sem=zr_sem.at[other],
            device_id=z_peers[other],
            device_id_type=MESH,
        )
        pl.when(z != other)(copy.wait)
    total = zrecv[0].astype(F32)
    for other in range(1, 8):
        total += zrecv[other].astype(F32)
    dw_out[...] = jnp.concatenate([total[0:6, :], total[8:14, :]], axis=1)


def sorting():
    source = np.arange(192).reshape(4, 8, 6).transpose(1, 0, 2).reshape(-1)
    return (source[:, None] == np.arange(192)[None, :]).astype(np.float32)


def shards(features, cotangent, w_query, w_key, w_value, neighbour, slot_mask, send_rows):
    whole = pl.BlockSpec(memory_space=VMEM)
    return pl.pallas_call(
        kernel,
        out_shape=(jax.ShapeDtypeStruct((ROWS, D), BF16), jax.ShapeDtypeStruct((6, D), F32)),
        in_specs=[pl.BlockSpec(memory_space=pl.ANY)] * 9,
        out_specs=(whole, whole),
        scratch_shapes=[
            VMEM((TABLE, D), BF16), VMEM((ROWS, D), BF16), VMEM((3, D, D), BF16), VMEM((SLOTS, ROWS), I32),
            VMEM((SLOTS, ROWS), I32), VMEM((4, HALO), I32), VMEM((192, 192), BF16),
            VMEM((ROWS, 4 * HALO), BF16), VMEM((ROWS, D), BF16), VMEM((TABLE, D), BF16), VMEM((TABLE, D), BF16),
            VMEM((TABLE, ROWS), F32), VMEM((HEADS, TABLE, ROWS), F32), VMEM((HEADS, TABLE, ROWS), F32),
            VMEM((HEADS, TABLE, ROWS), BF16), VMEM((HEADS, TABLE, ROWS), BF16),
            VMEM((ROWS, D), BF16), VMEM((TABLE, D), BF16), VMEM((TABLE, D), BF16), VMEM((3 * D, D), BF16),
            VMEM((2, 2, 16, 48, 256), BF16), VMEM((2, 16, 48, 256), BF16), VMEM((2, 16, 48, 256), BF16),
            VMEM((2, 15, 48, 256), BF16), VMEM((2, 32, D), F32), VMEM((8, 16, 256), BF16), VMEM((8, 16, 256), BF16),
            VMEM((ROWS, D), F32), VMEM((4, HALO, D), BF16), VMEM((4 * HALO, D), BF16),
            DMA((9,)), DMA((4,)), DMA((4,)), DMA((2,)), DMA((2,)), DMA((2, 15)), DMA((2, 15)),
            DMA((8,)), DMA((8,)), DMA((4,)), DMA((4,)),
        ],
        compiler_params=pltpu.CompilerParams(
            collective_id=0, has_side_effects=True, vmem_limit_bytes=60 * 1024 * 1024
        ),
        name="mesh_attention_backward",
    )(
        features, cotangent, w_query, w_key, w_value, neighbour.T, slot_mask.T, send_rows,
        jnp.asarray(sorting(), BF16),
    )


def solution(mesh):
    rows = P(("lon", "lat"), None)
    return jax.shard_map(
        shards,
        mesh=mesh,
        in_specs=(rows, rows, P(), P(), P(), rows, rows, rows),
        out_specs=(rows, rows),
        check_vma=False,
    )
```

```python
import jax
import jax.numpy as jnp
import numpy as np
from jax import lax
from jax.experimental import pallas as pl
from jax.experimental.pallas import tpu as pltpu
from jax.sharding import PartitionSpec as P

MESH = pl.DeviceIdType.MESH
F32, BF16, I32 = jnp.float32, jnp.bfloat16, jnp.int32
D, HEADS, SLOTS, ROWS, HALO = 512, 4, 16, 256, 128
HEAD = D // HEADS
TABLE = ROWS + 4 * HALO
SCALE = HEAD ** -0.5
NN = (((1,), (0,)), ((), ()))
NT = (((1,), (1,)), ((), ()))
TN = (((0,), (0,)), ((), ()))
VMEM = pltpu.VMEM
OFFSETS = sorted(
    ((dy, dx) for dy in range(4) for dx in range(4) if dy or dx),
    key=lambda at: -(min(at[0], 4 - at[0]) + min(at[1], 4 - at[1])),
)
DMA = pltpu.SemaphoreType.DMA


def dot(a, b, dims=NN):
    return lax.dot_general(a, b, dims, preferred_element_type=F32)


def kernel(
    feat, cot, w_query, w_key, w_value, nbr, msk, snd, perm,
    fg_out, dw_out,
    ftab, cot_v, w_v, nbr_v, msk_v, snd_v, perm_v,
    picked, q_v, k_v, v_v, bias, s_v, dp_v, p_v, ds_v, gq_v, gk_v, gv_v, dw_v,
    part, crecv, acc1, precv, acc2, zsend, zrecv, fg_own, fgh_s, fgh_r,
    in_sem, hs_sem, hr_sem, cs_sem, cr_sem, ps_sem, pr_sem, zs_sem, zr_sem, rs_sem, rr_sem,
):
    lon, lat = lax.axis_index("lon"), lax.axis_index("lat")
    z, core = lon // 4, lon % 2
    y, x = ((lon // 2) % 2) * 2 + lat // 4, lat % 4
    plane = y * 4 + x
    partner = (lon + 1 - 2 * core, lat)
    planes, plane_peers = [], []
    for dy, dx in OFFSETS:
        other_y, other_x = (y + dy) % 4, (x + dx) % 4
        planes.append(other_y * 4 + other_x)
        plane_peers.append((z * 4 + (other_y // 2) * 2 + core, (other_y % 2) * 4 + other_x))
    z_peers = [(other * 4 + lon % 4, lat) for other in range(8)]
    lat_lo, lat_hi = (lat + 7) % 8, (lat + 1) % 8
    far = ((lon + 31 + 2 * core) % 32, lat)
    sides = [partner, (lon, lat_lo), (lon, lat_hi), far]
    lands = (0, 2, 1, 3)

    def on_side(b, act):
        if b == 1:
            pl.when(lat > 0)(act)
        elif b == 2:
            pl.when(lat < 7)(act)
        else:
            act()

    def load(i, src, dst):
        copy = pltpu.make_async_copy(src, dst, in_sem.at[i])
        copy.start()
        return copy

    rows_in = [load(0, snd, snd_v), load(1, feat, ftab.at[pl.ds(0, ROWS)])]
    barrier = pltpu.get_barrier_semaphore()
    peers = [far, partner] + plane_peers + [(((z + d) % 8) * 4 + lon % 4, lat) for d in (4, 3, 5, 2, 6, 1, 7)]
    for peer in peers:
        pl.semaphore_signal(barrier, inc=1, device_id=peer, device_id_type=MESH)

    for copy in rows_in:
        copy.wait()
    weights_in = [load(2, w_query, w_v.at[0]), load(3, w_key, w_v.at[1]), load(4, w_value, w_v.at[2])]
    slots_in = [load(5, nbr, nbr_v), load(6, msk, msk_v)]
    rest_in = [load(7, cot, cot_v), load(8, perm, perm_v)]
    row_ids = lax.broadcasted_iota(I32, (ROWS, HALO), 0)
    below, above = snd_v[0:1, :], snd_v[1:2, :]
    lists = [jnp.where(core == 0, above, below), snd_v[2:3, :], snd_v[3:4, :], jnp.where(core == 0, below, above)]
    for b in (3, 1, 2, 0):
        chosen = (row_ids == lists[b]).astype(F32).astype(BF16)
        picked[:, b * HALO : (b + 1) * HALO] = chosen
        fgh_s[b] = dot(chosen, ftab[0:ROWS, :], TN).astype(BF16)
    pl.semaphore_wait(barrier, len(peers))
    halo = []
    for b in range(4):
        halo.append(
            pltpu.make_async_remote_copy(
                src_ref=fgh_s.at[b],
                dst_ref=ftab.at[pl.ds(ROWS + lands[b] * HALO, HALO)],
                send_sem=hs_sem.at[b],
                recv_sem=hr_sem.at[lands[b]],
                device_id=sides[b],
                device_id_type=MESH,
            )
        )
    for b in (3, 1, 2, 0):
        on_side(b, halo[b].start)

    for copy in weights_in:
        copy.wait()
    own = ftab[0:ROWS, :]
    q_v[...] = dot(own, w_v[0]).astype(BF16)
    k_v[0:ROWS, :] = dot(own, w_v[1]).astype(BF16)
    v_v[0:ROWS, :] = dot(own, w_v[2]).astype(BF16)
    for copy in slots_in:
        copy.wait()
    slot_ids = lax.broadcasted_iota(I32, (SLOTS, ROWS), 0)
    wanted = nbr_v[...]
    block = wanted // HALO
    moved = jnp.where(block == 2 + core, (3 - core) * HALO, jnp.where(block == 3 - core, (core - 1) * HALO, -HALO))
    wanted = jnp.where(wanted < ROWS, wanted, wanted + moved)
    wanted = jnp.where((msk_v[...] > 0) | (slot_ids == 0), wanted, -1)
    tile = 32
    for t in range(TABLE // tile):
        ids = lax.broadcasted_iota(I32, (tile, ROWS), 0) + t * tile
        b = jnp.full((tile, ROWS), -1e30, F32)
        for j in range(SLOTS):
            b = jnp.where(ids == wanted[j : j + 1, :], 0.0, b)
        bias[t * tile : (t + 1) * tile, :] = b
    for copy in rest_in:
        copy.wait()

    step = 64
    tops = [jnp.full((8, ROWS), -3e38, F32) for _ in range(HEADS)]

    def products(lo, hi):
        for h in range(HEADS):
            cols = slice(h * HEAD, (h + 1) * HEAD)
            s_v[h, lo:hi, :] = dot(k_v[lo:hi, cols], q_v[:, cols], NT)
            dp_v[h, lo:hi, :] = dot(v_v[lo:hi, cols], cot_v[:, cols], NT)
            for t in range(lo, hi, step):
                s = s_v[h, t : t + step, :] + bias[t : t + step, :]
                s_v[h, t : t + step, :] = s
                tops[h] = jnp.maximum(tops[h], jnp.max(s.reshape(step // 8, 8, ROWS), axis=0))

    def softmax_start(h, lo, hi, top):
        total = jnp.zeros((8, ROWS), F32)
        inner = jnp.zeros((8, ROWS), F32)
        for t in range(lo, hi, step):
            e = jnp.exp((s_v[h, t : t + step, :] - top) * SCALE)
            s_v[h, t : t + step, :] = e
            total += jnp.sum(e.reshape(step // 8, 8, ROWS), axis=0)
            inner += jnp.sum((e * dp_v[h, t : t + step, :]).reshape(step // 8, 8, ROWS), axis=0)
        return jnp.sum(total, axis=0, keepdims=True), jnp.sum(inner, axis=0, keepdims=True)

    products(0, ROWS)

    for b in range(4):
        lo, hi = ROWS + b * HALO, ROWS + (b + 1) * HALO
        if b == 3:
            early = [jnp.max(tops[h], axis=0, keepdims=True) for h in range(HEADS)]
            sums = [softmax_start(h, 0, lo, early[h]) for h in range(HEADS)]
        on_side(b, halo[lands[b]].wait_recv)
        if b in (1, 2):

            @pl.when(lat == (0 if b == 1 else 7))
            def _():
                ftab[lo:hi, :] = jnp.zeros((HALO, D), BF16)

        rows = ftab[lo:hi, :]
        k_v[lo:hi, :] = dot(rows, w_v[1]).astype(BF16)
        v_v[lo:hi, :] = dot(rows, w_v[2]).astype(BF16)
        products(lo, hi)

    last = TABLE - HALO
    for h in range(HEADS):
        cols = slice(h * HEAD, (h + 1) * HEAD)
        top = jnp.max(tops[h], axis=0, keepdims=True)
        fall = jnp.exp((early[h] - top) * SCALE)
        total, inner = softmax_start(h, last, TABLE, top)
        total += sums[h][0] * fall
        inner += sums[h][1] * fall
        inverse = 1.0 / total
        inner *= inverse
        fall *= inverse
        for t in range(0, TABLE, step):
            p = s_v[h, t : t + step, :] * (fall if t < last else inverse)
            p_v[h, t : t + step, :] = p.astype(BF16)
            ds_v[h, t : t + step, :] = (p * (dp_v[h, t : t + step, :] - inner) * SCALE).astype(BF16)
        gq_v[:, cols] = dot(ds_v[h], k_v[:, cols], TN).astype(BF16)
        if h < 2:
            gk_v[:, cols] = dot(ds_v[h], q_v[:, cols]).astype(BF16)

    def to_partner(c):
        for half in range(2):
            for y_hi in range(2):
                rows = jnp.concatenate(
                    [dw_v[pl.ds((c * 4 + zz) * 192 + y_hi * 96 + half * 48, 48), :] for zz in range(4)], axis=0
                )
                sorted_rows = dot(perm_v[...], rows)
                for k in range(8):
                    block = sorted_rows[k * 24 : (k + 1) * 24, :]
                    block = jnp.concatenate([block[:, 0:256], block[:, 256:512]], axis=0)
                    part[c, half, y_hi * 8 + k] = block.astype(BF16)
        copy = pltpu.make_async_remote_copy(
            src_ref=part.at[c, 1 - core],
            dst_ref=crecv.at[c],
            send_sem=cs_sem.at[c],
            recv_sem=cr_sem.at[c],
            device_id=partner,
            device_id_type=MESH,
        )
        copy.start()
        return copy

    def to_plane(c, from_partner):
        from_partner.wait_recv()
        copies = []
        for i, other in enumerate(planes):
            acc1[c, other] = (part[c, core, other].astype(F32) + crecv[c, other].astype(F32)).astype(BF16)
            copy = pltpu.make_async_remote_copy(
                src_ref=acc1.at[c, other],
                dst_ref=precv.at[c, i],
                send_sem=ps_sem.at[c, i],
                recv_sem=pr_sem.at[c, i],
                device_id=plane_peers[i],
                device_id_type=MESH,
            )
            copy.start()
            copies.append(copy)
        return copies

    def to_z(c, from_plane):
        total = part[c, core, plane].astype(F32) + crecv[c, plane].astype(F32)
        for i, copy in enumerate(from_plane):
            copy.wait_recv()
            total += precv[c, i].astype(F32)
        acc2[c, 0:24, :] = jnp.concatenate([total[0:24, :], total[24:48, :]], axis=1)
        acc2[c, 24:32, :] = jnp.zeros((8, D), F32)
        copies = []
        for zz in range(4):
            other = c * 4 + zz
            rows = acc2[c, zz * 6 : zz * 6 + 8, :]
            zsend[other] = jnp.concatenate([rows[:, 0:256], rows[:, 256:512]], axis=0).astype(BF16)
            copy = pltpu.make_async_remote_copy(
                src_ref=zsend.at[other],
                dst_ref=zrecv.at[z],
                send_sem=zs_sem.at[other],
                recv_sem=zr_sem.at[z],
                device_id=z_peers[other],
                device_id_type=MESH,
            )
            pl.when(z != other)(copy.start)
        return copies

    dw_v[0:D, :] = dot(gq_v[...], own, TN).astype(BF16)
    dw_v[D : D + 256, :] = dot(gk_v[:, 0:256], ftab[...], TN).astype(BF16)
    core_a = to_partner(0)
    for h in range(HEADS):
        cols = slice(h * HEAD, (h + 1) * HEAD)
        gv_v[:, cols] = dot(p_v[h], cot_v[:, cols]).astype(BF16)
        if h >= 2:
            gk_v[:, cols] = dot(ds_v[h], q_v[:, cols]).astype(BF16)
    plane_a = to_plane(0, core_a)
    dw_v[D + 256 : 2 * D, :] = dot(gk_v[:, 256:512], ftab[...], TN).astype(BF16)
    dw_v[2 * D : 3 * D, :] = dot(gv_v[...], ftab[...], TN).astype(BF16)
    core_b = to_partner(1)
    fg_own[...] = (
        dot(gq_v[...], w_v[0], NT) + dot(gk_v[0:ROWS, :], w_v[1], NT) + dot(gv_v[0:ROWS, :], w_v[2], NT)
    )
    plane_b = to_plane(1, core_b)

    back = []
    for b in range(4):
        back.append(
            pltpu.make_async_remote_copy(
                src_ref=fgh_s.at[b],
                dst_ref=fgh_r.at[pl.ds(lands[b] * HALO, HALO)],
                send_sem=rs_sem.at[b],
                recv_sem=rr_sem.at[lands[b]],
                device_id=sides[b],
                device_id_type=MESH,
            )
        )
    for b in (3, 1, 2, 0):
        on_side(b, halo[b].wait_send)
        rows = slice(ROWS + b * HALO, ROWS + (b + 1) * HALO)
        fgh_s[b] = (dot(gk_v[rows, :], w_v[1], NT) + dot(gv_v[rows, :], w_v[2], NT)).astype(BF16)
    to_z(0, plane_a)
    for b in (3, 1, 2, 0):
        on_side(b, back[b].start)
    to_z(1, plane_b)

    for b in range(4):
        on_side(lands[b], back[b].wait_recv)
        on_side(b, back[b].wait_send)

    @pl.when(lat == 0)
    def _():
        fgh_r[1 * HALO : 2 * HALO, :] = jnp.zeros((HALO, D), BF16)

    @pl.when(lat == 7)
    def _():
        fgh_r[2 * HALO : 3 * HALO, :] = jnp.zeros((HALO, D), BF16)

    fg_out[...] = (fg_own[...] + dot(picked[...], fgh_r[...])).astype(BF16)

    for copy in [core_a, core_b] + plane_a + plane_b:
        copy.wait_send()
    zrecv[z] = zsend[z]
    for other in range(8):
        copy = pltpu.make_async_remote_copy(
            src_ref=zsend.at[other],
            dst_ref=zrecv.at[other],
            send_sem=zs_sem.at[other],
            recv_sem=zr_sem.at[other],
            device_id=z_peers[other],
            device_id_type=MESH,
        )
        pl.when(z != other)(copy.wait)
    total = zrecv[0].astype(F32)
    for other in range(1, 8):
        total += zrecv[other].astype(F32)
    dw_out[...] = jnp.concatenate([total[0:6, :], total[8:14, :]], axis=1)


def sorting():
    source = np.arange(192).reshape(4, 8, 6).transpose(1, 0, 2).reshape(-1)
    return (source[:, None] == np.arange(192)[None, :]).astype(np.float32)


def shards(features, cotangent, w_query, w_key, w_value, neighbour, slot_mask, send_rows):
    whole = pl.BlockSpec(memory_space=VMEM)
    return pl.pallas_call(
        kernel,
        out_shape=(jax.ShapeDtypeStruct((ROWS, D), BF16), jax.ShapeDtypeStruct((6, D), F32)),
        in_specs=[pl.BlockSpec(memory_space=pl.ANY)] * 9,
        out_specs=(whole, whole),
        scratch_shapes=[
            VMEM((TABLE, D), BF16), VMEM((ROWS, D), BF16), VMEM((3, D, D), BF16), VMEM((SLOTS, ROWS), I32),
            VMEM((SLOTS, ROWS), I32), VMEM((4, HALO), I32), VMEM((192, 192), BF16),
            VMEM((ROWS, 4 * HALO), BF16), VMEM((ROWS, D), BF16), VMEM((TABLE, D), BF16), VMEM((TABLE, D), BF16),
            VMEM((TABLE, ROWS), F32), VMEM((HEADS, TABLE, ROWS), F32), VMEM((HEADS, TABLE, ROWS), F32),
            VMEM((HEADS, TABLE, ROWS), BF16), VMEM((HEADS, TABLE, ROWS), BF16),
            VMEM((ROWS, D), BF16), VMEM((TABLE, D), BF16), VMEM((TABLE, D), BF16), VMEM((3 * D, D), BF16),
            VMEM((2, 2, 16, 48, 256), BF16), VMEM((2, 16, 48, 256), BF16), VMEM((2, 16, 48, 256), BF16),
            VMEM((2, 15, 48, 256), BF16), VMEM((2, 32, D), F32), VMEM((8, 16, 256), BF16), VMEM((8, 16, 256), BF16),
            VMEM((ROWS, D), F32), VMEM((4, HALO, D), BF16), VMEM((4 * HALO, D), BF16),
            DMA((9,)), DMA((4,)), DMA((4,)), DMA((2,)), DMA((2,)), DMA((2, 15)), DMA((2, 15)),
            DMA((8,)), DMA((8,)), DMA((4,)), DMA((4,)),
        ],
        compiler_params=pltpu.CompilerParams(
            collective_id=0, has_side_effects=True, vmem_limit_bytes=60 * 1024 * 1024
        ),
        name="mesh_attention_backward",
    )(
        features, cotangent, w_query, w_key, w_value, neighbour.T, slot_mask.T, send_rows,
        jnp.asarray(sorting(), BF16),
    )


def solution(mesh):
    rows = P(("lon", "lat"), None)
    return jax.shard_map(
        shards,
        mesh=mesh,
        in_specs=(rows, rows, P(), P(), P(), rows, rows, rows),
        out_specs=(rows, rows),
        check_vma=False,
    )
```

```python
import jax
import jax.numpy as jnp
import numpy as np
from jax import lax
from jax.experimental import pallas as pl
from jax.experimental.pallas import tpu as pltpu
from jax.sharding import PartitionSpec as P

MESH = pl.DeviceIdType.MESH
F32, BF16, I32 = jnp.float32, jnp.bfloat16, jnp.int32
D, HEADS, SLOTS, ROWS, HALO = 512, 4, 16, 256, 128
HEAD = D // HEADS
TABLE = ROWS + 4 * HALO
SCALE = HEAD ** -0.5
NN = (((1,), (0,)), ((), ()))
NT = (((1,), (1,)), ((), ()))
TN = (((0,), (0,)), ((), ()))
VMEM = pltpu.VMEM
OFFSETS = sorted(
    ((dy, dx) for dy in range(4) for dx in range(4) if dy or dx),
    key=lambda at: -(min(at[0], 4 - at[0]) + min(at[1], 4 - at[1])),
)
DMA = pltpu.SemaphoreType.DMA


def dot(a, b, dims=NN):
    return lax.dot_general(a, b, dims, preferred_element_type=F32)


def kernel(
    feat, cot, w_query, w_key, w_value, nbr, msk, snd, perm,
    fg_out, dw_out,
    ftab, cot_v, w_v, nbr_v, msk_v, snd_v, perm_v,
    picked, q_v, k_v, v_v, bias, s_v, dp_v, p_v, ds_v, gq_v, gk_v, gv_v, dw_v,
    part, crecv, acc1, precv, acc2, zsend, zrecv, fg_own, fgh_s, fgh_r,
    in_sem, hs_sem, hr_sem, cs_sem, cr_sem, ps_sem, pr_sem, zs_sem, zr_sem, rs_sem, rr_sem,
    result, out_sem,
):
    lon, lat = lax.axis_index("lon"), lax.axis_index("lat")
    z, core = lon // 4, lon % 2
    y, x = ((lon // 2) % 2) * 2 + lat // 4, lat % 4
    plane = y * 4 + x
    partner = (lon + 1 - 2 * core, lat)
    planes, plane_peers = [], []
    for dy, dx in OFFSETS:
        other_y, other_x = (y + dy) % 4, (x + dx) % 4
        planes.append(other_y * 4 + other_x)
        plane_peers.append((z * 4 + (other_y // 2) * 2 + core, (other_y % 2) * 4 + other_x))
    z_peers = [(other * 4 + lon % 4, lat) for other in range(8)]
    lat_lo, lat_hi = (lat + 7) % 8, (lat + 1) % 8
    far = ((lon + 31 + 2 * core) % 32, lat)
    sides = [partner, (lon, lat_lo), (lon, lat_hi), far]
    lands = (0, 2, 1, 3)

    def on_side(b, act):
        if b == 1:
            pl.when(lat > 0)(act)
        elif b == 2:
            pl.when(lat < 7)(act)
        else:
            act()

    def load(i, src, dst):
        copy = pltpu.make_async_copy(src, dst, in_sem.at[i])
        copy.start()
        return copy

    rows_in = [load(0, snd, snd_v)]
    for i in range(4):
        quarter = pl.ds(i * 64, 64)
        rows_in.append(load(9 + i, feat.at[quarter], ftab.at[quarter]))
    barrier = pltpu.get_barrier_semaphore()
    peers = [far, partner] + plane_peers + [(((z + d) % 8) * 4 + lon % 4, lat) for d in (4, 3, 5, 2, 6, 1, 7)]
    for peer in peers:
        pl.semaphore_signal(barrier, inc=1, device_id=peer, device_id_type=MESH)

    for copy in rows_in:
        copy.wait()
    row_ids = lax.broadcasted_iota(I32, (ROWS, HALO), 0)
    below, above = snd_v[0:1, :], snd_v[1:2, :]
    lists = [jnp.where(core == 0, above, below), snd_v[2:3, :], snd_v[3:4, :], jnp.where(core == 0, below, above)]
    for b in (3, 1, 2, 0):
        chosen = (row_ids == lists[b]).astype(F32).astype(BF16)
        picked[:, b * HALO : (b + 1) * HALO] = chosen
        fgh_s[b] = dot(chosen, ftab[0:ROWS, :], TN).astype(BF16)
    pl.semaphore_wait(barrier, len(peers))
    halo = []
    for b in range(4):
        halo.append(
            pltpu.make_async_remote_copy(
                src_ref=fgh_s.at[b],
                dst_ref=ftab.at[pl.ds(ROWS + lands[b] * HALO, HALO)],
                send_sem=hs_sem.at[b],
                recv_sem=hr_sem.at[lands[b]],
                device_id=sides[b],
                device_id_type=MESH,
            )
        )
    for b in (3, 1, 2, 0):
        on_side(b, halo[b].start)

    weights_in = [load(2, w_query, w_v.at[0]), load(3, w_key, w_v.at[1]), load(4, w_value, w_v.at[2])]
    slots_in = [load(5, nbr, nbr_v), load(6, msk, msk_v)]
    rest_in = [load(7, cot, cot_v), load(8, perm, perm_v)]
    for copy in weights_in:
        copy.wait()
    own = ftab[0:ROWS, :]
    q_v[...] = dot(own, w_v[0]).astype(BF16)
    k_v[0:ROWS, :] = dot(own, w_v[1]).astype(BF16)
    v_v[0:ROWS, :] = dot(own, w_v[2]).astype(BF16)
    for copy in slots_in:
        copy.wait()
    slot_ids = lax.broadcasted_iota(I32, (SLOTS, ROWS), 0)
    wanted = nbr_v[...]
    block = wanted // HALO
    moved = jnp.where(block == 2 + core, (3 - core) * HALO, jnp.where(block == 3 - core, (core - 1) * HALO, -HALO))
    wanted = jnp.where(wanted < ROWS, wanted, wanted + moved)
    wanted = jnp.where((msk_v[...] > 0) | (slot_ids == 0), wanted, -1)
    tile = 32
    for t in range(TABLE // tile):
        ids = lax.broadcasted_iota(I32, (tile, ROWS), 0) + t * tile
        b = jnp.full((tile, ROWS), -1e30, F32)
        for j in range(SLOTS):
            b = jnp.where(ids == wanted[j : j + 1, :], 0.0, b)
        bias[t * tile : (t + 1) * tile, :] = b
    for copy in rest_in:
        copy.wait()

    step = 64
    tops = [jnp.full((8, ROWS), -3e38, F32) for _ in range(HEADS)]

    def products(lo, hi):
        for h in range(HEADS):
            cols = slice(h * HEAD, (h + 1) * HEAD)
            s_v[h, lo:hi, :] = dot(k_v[lo:hi, cols], q_v[:, cols], NT)
            dp_v[h, lo:hi, :] = dot(v_v[lo:hi, cols], cot_v[:, cols], NT)
            for t in range(lo, hi, step):
                s = s_v[h, t : t + step, :] + bias[t : t + step, :]
                s_v[h, t : t + step, :] = s
                tops[h] = jnp.maximum(tops[h], jnp.max(s.reshape(step // 8, 8, ROWS), axis=0))

    def softmax_start(h, lo, hi, top):
        total = jnp.zeros((8, ROWS), F32)
        inner = jnp.zeros((8, ROWS), F32)
        for t in range(lo, hi, step):
            e = jnp.exp((s_v[h, t : t + step, :] - top) * SCALE)
            s_v[h, t : t + step, :] = e
            total += jnp.sum(e.reshape(step // 8, 8, ROWS), axis=0)
            inner += jnp.sum((e * dp_v[h, t : t + step, :]).reshape(step // 8, 8, ROWS), axis=0)
        return jnp.sum(total, axis=0, keepdims=True), jnp.sum(inner, axis=0, keepdims=True)

    products(0, ROWS)

    for b in range(4):
        lo, hi = ROWS + b * HALO, ROWS + (b + 1) * HALO
        if b == 3:
            early = [jnp.max(tops[h], axis=0, keepdims=True) for h in range(HEADS)]
            sums = [softmax_start(h, 0, lo, early[h]) for h in range(HEADS)]
        on_side(b, halo[lands[b]].wait_recv)
        if b in (1, 2):

            @pl.when(lat == (0 if b == 1 else 7))
            def _():
                ftab[lo:hi, :] = jnp.zeros((HALO, D), BF16)

        rows = ftab[lo:hi, :]
        k_v[lo:hi, :] = dot(rows, w_v[1]).astype(BF16)
        v_v[lo:hi, :] = dot(rows, w_v[2]).astype(BF16)
        products(lo, hi)

    last = TABLE - HALO
    for h in range(HEADS):
        cols = slice(h * HEAD, (h + 1) * HEAD)
        top = jnp.max(tops[h], axis=0, keepdims=True)
        fall = jnp.exp((early[h] - top) * SCALE)
        total, inner = softmax_start(h, last, TABLE, top)
        total += sums[h][0] * fall
        inner += sums[h][1] * fall
        inverse = 1.0 / total
        inner *= inverse
        fall *= inverse
        for t in range(0, TABLE, step):
            p = s_v[h, t : t + step, :] * (fall if t < last else inverse)
            p_v[h, t : t + step, :] = p.astype(BF16)
            ds_v[h, t : t + step, :] = (p * (dp_v[h, t : t + step, :] - inner) * SCALE).astype(BF16)
        gq_v[:, cols] = dot(ds_v[h], k_v[:, cols], TN).astype(BF16)
        if h < 2:
            gk_v[:, cols] = dot(ds_v[h], q_v[:, cols]).astype(BF16)

    def to_partner(c):
        for half in range(2):
            for y_hi in range(2):
                rows = jnp.concatenate(
                    [dw_v[pl.ds((c * 4 + zz) * 192 + y_hi * 96 + half * 48, 48), :] for zz in range(4)], axis=0
                )
                sorted_rows = dot(perm_v[...], rows)
                for k in range(8):
                    block = sorted_rows[k * 24 : (k + 1) * 24, :]
                    block = jnp.concatenate([block[:, 0:256], block[:, 256:512]], axis=0)
                    part[c, half, y_hi * 8 + k] = block.astype(BF16)
        copy = pltpu.make_async_remote_copy(
            src_ref=part.at[c, 1 - core],
            dst_ref=crecv.at[c],
            send_sem=cs_sem.at[c],
            recv_sem=cr_sem.at[c],
            device_id=partner,
            device_id_type=MESH,
        )
        copy.start()
        return copy

    def to_plane(c, from_partner):
        from_partner.wait_recv()
        copies = []
        for i, other in enumerate(planes):
            acc1[c, other] = (part[c, core, other].astype(F32) + crecv[c, other].astype(F32)).astype(BF16)
            copy = pltpu.make_async_remote_copy(
                src_ref=acc1.at[c, other],
                dst_ref=precv.at[c, i],
                send_sem=ps_sem.at[c, i],
                recv_sem=pr_sem.at[c, i],
                device_id=plane_peers[i],
                device_id_type=MESH,
            )
            copy.start()
            copies.append(copy)
        return copies

    def to_z(c, from_plane):
        total = part[c, core, plane].astype(F32) + crecv[c, plane].astype(F32)
        for i, copy in enumerate(from_plane):
            copy.wait_recv()
            total += precv[c, i].astype(F32)
        acc2[c, 0:24, :] = jnp.concatenate([total[0:24, :], total[24:48, :]], axis=1)
        acc2[c, 24:32, :] = jnp.zeros((8, D), F32)
        copies = []
        for zz in range(4):
            other = c * 4 + zz
            rows = acc2[c, zz * 6 : zz * 6 + 8, :]
            zsend[other] = jnp.concatenate([rows[:, 0:256], rows[:, 256:512]], axis=0).astype(BF16)
            copy = pltpu.make_async_remote_copy(
                src_ref=zsend.at[other],
                dst_ref=zrecv.at[z],
                send_sem=zs_sem.at[other],
                recv_sem=zr_sem.at[z],
                device_id=z_peers[other],
                device_id_type=MESH,
            )
            pl.when(z != other)(copy.start)
        return copies

    dw_v[0:D, :] = dot(gq_v[...], own, TN).astype(BF16)
    dw_v[D : D + 256, :] = dot(gk_v[:, 0:256], ftab[...], TN).astype(BF16)
    core_a = to_partner(0)
    for h in range(HEADS):
        cols = slice(h * HEAD, (h + 1) * HEAD)
        gv_v[:, cols] = dot(p_v[h], cot_v[:, cols]).astype(BF16)
        if h >= 2:
            gk_v[:, cols] = dot(ds_v[h], q_v[:, cols]).astype(BF16)
    plane_a = to_plane(0, core_a)
    dw_v[D + 256 : 2 * D, :] = dot(gk_v[:, 256:512], ftab[...], TN).astype(BF16)
    dw_v[2 * D : 3 * D, :] = dot(gv_v[...], ftab[...], TN).astype(BF16)
    core_b = to_partner(1)
    plane_b = to_plane(1, core_b)
    fg_own[...] = (
        dot(gq_v[...], w_v[0], NT) + dot(gk_v[0:ROWS, :], w_v[1], NT) + dot(gv_v[0:ROWS, :], w_v[2], NT)
    )

    back = []
    for b in range(4):
        back.append(
            pltpu.make_async_remote_copy(
                src_ref=fgh_s.at[b],
                dst_ref=fgh_r.at[pl.ds(lands[b] * HALO, HALO)],
                send_sem=rs_sem.at[b],
                recv_sem=rr_sem.at[lands[b]],
                device_id=sides[b],
                device_id_type=MESH,
            )
        )
    for b in (3, 1, 2, 0):
        on_side(b, halo[b].wait_send)
        rows = slice(ROWS + b * HALO, ROWS + (b + 1) * HALO)
        fgh_s[b] = (dot(gk_v[rows, :], w_v[1], NT) + dot(gv_v[rows, :], w_v[2], NT)).astype(BF16)
    to_z(0, plane_a)
    for b in (3, 1, 2, 0):
        on_side(b, back[b].start)
    to_z(1, plane_b)

    for b in range(3):
        on_side(lands[b], back[b].wait_recv)

    @pl.when(lat == 0)
    def _():
        fgh_r[1 * HALO : 2 * HALO, :] = jnp.zeros((HALO, D), BF16)

    @pl.when(lat == 7)
    def _():
        fgh_r[2 * HALO : 3 * HALO, :] = jnp.zeros((HALO, D), BF16)

    fg_own[...] += dot(picked[:, 0 : 3 * HALO], fgh_r[0 : 3 * HALO, :])

    for copy in [core_a, core_b] + plane_a + plane_b:
        copy.wait_send()
    zrecv[z] = zsend[z]
    for other in range(8):
        copy = pltpu.make_async_remote_copy(
            src_ref=zsend.at[other],
            dst_ref=zrecv.at[other],
            send_sem=zs_sem.at[other],
            recv_sem=zr_sem.at[other],
            device_id=z_peers[other],
            device_id_type=MESH,
        )
        pl.when(z != other)(copy.wait)
    total = zrecv[0].astype(F32)
    for other in range(1, 8):
        total += zrecv[other].astype(F32)
    dw_out[...] = jnp.concatenate([total[0:6, :], total[8:14, :]], axis=1)
    for b in range(4):
        on_side(b, back[b].wait_send)
    back[3].wait_recv()
    fg_copies = []
    for i in range(2):
        rows = slice(i * 128, (i + 1) * 128)
        result[rows, :] = (fg_own[rows, :] + dot(picked[rows, 3 * HALO :], fgh_r[3 * HALO :, :])).astype(BF16)
        fg_copies.append(pltpu.make_async_copy(result.at[pl.ds(i * 128, 128)], fg_out.at[pl.ds(i * 128, 128)], out_sem.at[i]))
        fg_copies[i].start()
    for copy in fg_copies:
        copy.wait()


def sorting():
    source = np.arange(192).reshape(4, 8, 6).transpose(1, 0, 2).reshape(-1)
    return (source[:, None] == np.arange(192)[None, :]).astype(np.float32)


def handing_on(fg, dw, fg_out, dw_out):
    fg_out[...] = fg[...]
    dw_out[...] = dw[...]


def shards(features, cotangent, w_query, w_key, w_value, neighbour, slot_mask, send_rows):
    whole = pl.BlockSpec(memory_space=VMEM)
    shapes = (jax.ShapeDtypeStruct((ROWS, D), BF16), jax.ShapeDtypeStruct((6, D), F32))
    results = pl.pallas_call(
        kernel,
        out_shape=shapes,
        in_specs=[pl.BlockSpec(memory_space=pl.ANY)] * 9,
        out_specs=(pl.BlockSpec(memory_space=pl.ANY), whole),
        scratch_shapes=[
            VMEM((TABLE, D), BF16), VMEM((ROWS, D), BF16), VMEM((3, D, D), BF16), VMEM((SLOTS, ROWS), I32),
            VMEM((SLOTS, ROWS), I32), VMEM((4, HALO), I32), VMEM((192, 192), BF16),
            VMEM((ROWS, 4 * HALO), BF16), VMEM((ROWS, D), BF16), VMEM((TABLE, D), BF16), VMEM((TABLE, D), BF16),
            VMEM((TABLE, ROWS), F32), VMEM((HEADS, TABLE, ROWS), F32), VMEM((HEADS, TABLE, ROWS), F32),
            VMEM((HEADS, TABLE, ROWS), BF16), VMEM((HEADS, TABLE, ROWS), BF16),
            VMEM((ROWS, D), BF16), VMEM((TABLE, D), BF16), VMEM((TABLE, D), BF16), VMEM((3 * D, D), BF16),
            VMEM((2, 2, 16, 48, 256), BF16), VMEM((2, 16, 48, 256), BF16), VMEM((2, 16, 48, 256), BF16),
            VMEM((2, 15, 48, 256), BF16), VMEM((2, 32, D), F32), VMEM((8, 16, 256), BF16), VMEM((8, 16, 256), BF16),
            VMEM((ROWS, D), F32), VMEM((4, HALO, D), BF16), VMEM((4 * HALO, D), BF16),
            DMA((13,)), DMA((4,)), DMA((4,)), DMA((2,)), DMA((2,)), DMA((2, 15)), DMA((2, 15)),
            DMA((8,)), DMA((8,)), DMA((4,)), DMA((4,)),
            VMEM((ROWS, D), BF16), DMA((2,)),
        ],
        compiler_params=pltpu.CompilerParams(
            collective_id=0, has_side_effects=True, vmem_limit_bytes=60 * 1024 * 1024
        ),
        name="mesh_attention_backward",
    )(
        features, cotangent, w_query, w_key, w_value, neighbour.T, slot_mask.T, send_rows,
        jnp.asarray(sorting(), BF16),
    )
    return pl.pallas_call(
        handing_on,
        out_shape=shapes,
        in_specs=[whole] * 2,
        out_specs=(whole,) * 2,
        compiler_params=pltpu.CompilerParams(vmem_limit_bytes=60 * 1024 * 1024),
        name="handing_on",
    )(*results)


def solution(mesh):
    rows = P(("lon", "lat"), None)
    return jax.shard_map(
        shards,
        mesh=mesh,
        in_specs=(rows, rows, P(), P(), P(), rows, rows, rows),
        out_specs=(rows, rows),
        check_vma=False,
    )
```

```python
import jax
import jax.numpy as jnp
import numpy as np
from jax import lax
from jax.experimental import pallas as pl
from jax.experimental.pallas import tpu as pltpu
from jax.sharding import PartitionSpec as P

MESH = pl.DeviceIdType.MESH
F32, BF16, I32 = jnp.float32, jnp.bfloat16, jnp.int32
D, HEADS, SLOTS, ROWS, HALO = 512, 4, 16, 256, 128
HEAD = D // HEADS
TABLE = ROWS + 4 * HALO
SCALE = HEAD ** -0.5
NN = (((1,), (0,)), ((), ()))
NT = (((1,), (1,)), ((), ()))
TN = (((0,), (0,)), ((), ()))
VMEM = pltpu.VMEM
OFFSETS = sorted(
    ((dy, dx) for dy in range(4) for dx in range(4) if dy or dx),
    key=lambda at: -(min(at[0], 4 - at[0]) + min(at[1], 4 - at[1])),
)
DMA = pltpu.SemaphoreType.DMA


def dot(a, b, dims=NN):
    return lax.dot_general(a, b, dims, preferred_element_type=F32)


def kernel(
    feat, cot, w_query, w_key, w_value, nbr, msk, snd, perm,
    fg_out, dw_out,
    ftab, cot_v, w_v, nbr_v, msk_v, snd_v, perm_v,
    picked, q_v, k_v, v_v, bias, s_v, dp_v, p_v, ds_v, gq_v, gk_v, gv_v, dw_v,
    part, crecv, acc1, precv, acc2, zsend, zrecv, fg_own, fgh_s, fgh_r,
    in_sem, hs_sem, hr_sem, cs_sem, cr_sem, ps_sem, pr_sem, zs_sem, zr_sem, rs_sem, rr_sem,
):
    lon, lat = lax.axis_index("lon"), lax.axis_index("lat")
    z, core = lon // 4, lon % 2
    y, x = ((lon // 2) % 2) * 2 + lat // 4, lat % 4
    plane = y * 4 + x
    partner = (lon + 1 - 2 * core, lat)
    planes, plane_peers = [], []
    for dy, dx in OFFSETS:
        other_y, other_x = (y + dy) % 4, (x + dx) % 4
        planes.append(other_y * 4 + other_x)
        plane_peers.append((z * 4 + (other_y // 2) * 2 + core, (other_y % 2) * 4 + other_x))
    z_peers = [(other * 4 + lon % 4, lat) for other in range(8)]
    lat_lo, lat_hi = (lat + 7) % 8, (lat + 1) % 8
    far = ((lon + 31 + 2 * core) % 32, lat)
    sides = [partner, (lon, lat_lo), (lon, lat_hi), far]
    lands = (0, 2, 1, 3)

    def on_side(b, act):
        if b == 1:
            pl.when(lat > 0)(act)
        elif b == 2:
            pl.when(lat < 7)(act)
        else:
            act()

    def load(i, src, dst):
        copy = pltpu.make_async_copy(src, dst, in_sem.at[i])
        copy.start()
        return copy

    rows_in = [load(0, snd, snd_v), load(1, feat, ftab.at[pl.ds(0, ROWS)])]
    barrier = pltpu.get_barrier_semaphore()
    peers = [far, partner] + plane_peers + [(((z + d) % 8) * 4 + lon % 4, lat) for d in (4, 3, 5, 2, 6, 1, 7)]
    for peer in peers:
        pl.semaphore_signal(barrier, inc=1, device_id=peer, device_id_type=MESH)

    for copy in rows_in:
        copy.wait()
    weights_in = [load(2, w_query, w_v.at[0]), load(3, w_key, w_v.at[1]), load(4, w_value, w_v.at[2])]
    slots_in = [load(5, nbr, nbr_v), load(6, msk, msk_v)]
    rest_in = [load(7, cot, cot_v), load(8, perm, perm_v)]
    row_ids = lax.broadcasted_iota(I32, (ROWS, HALO), 0)
    below, above = snd_v[0:1, :], snd_v[1:2, :]
    lists = [jnp.where(core == 0, above, below), snd_v[2:3, :], snd_v[3:4, :], jnp.where(core == 0, below, above)]
    for b in (3, 1, 2, 0):
        chosen = (row_ids == lists[b]).astype(F32).astype(BF16)
        picked[:, b * HALO : (b + 1) * HALO] = chosen
        fgh_s[b] = dot(chosen, ftab[0:ROWS, :], TN).astype(BF16)
    pl.semaphore_wait(barrier, len(peers))
    halo = []
    for b in range(4):
        halo.append(
            pltpu.make_async_remote_copy(
                src_ref=fgh_s.at[b],
                dst_ref=ftab.at[pl.ds(ROWS + lands[b] * HALO, HALO)],
                send_sem=hs_sem.at[b],
                recv_sem=hr_sem.at[lands[b]],
                device_id=sides[b],
                device_id_type=MESH,
            )
        )
    for b in (3, 1, 2, 0):
        on_side(b, halo[b].start)

    for copy in weights_in:
        copy.wait()
    own = ftab[0:ROWS, :]
    q_v[...] = dot(own, w_v[0]).astype(BF16)
    k_v[0:ROWS, :] = dot(own, w_v[1]).astype(BF16)
    v_v[0:ROWS, :] = dot(own, w_v[2]).astype(BF16)
    for copy in slots_in:
        copy.wait()
    slot_ids = lax.broadcasted_iota(I32, (SLOTS, ROWS), 0)
    wanted = nbr_v[...]
    block = wanted // HALO
    moved = jnp.where(block == 2 + core, (3 - core) * HALO, jnp.where(block == 3 - core, (core - 1) * HALO, -HALO))
    wanted = jnp.where(wanted < ROWS, wanted, wanted + moved)
    wanted = jnp.where((msk_v[...] > 0) | (slot_ids == 0), wanted, -1)
    tile = 32
    for t in range(TABLE // tile):
        ids = lax.broadcasted_iota(I32, (tile, ROWS), 0) + t * tile
        b = jnp.full((tile, ROWS), -1e30, F32)
        for j in range(SLOTS):
            b = jnp.where(ids == wanted[j : j + 1, :], 0.0, b)
        bias[t * tile : (t + 1) * tile, :] = b
    for copy in rest_in:
        copy.wait()

    step = 64
    tops = [jnp.full((8, ROWS), -3e38, F32) for _ in range(HEADS)]

    def products(lo, hi):
        for h in range(HEADS):
            cols = slice(h * HEAD, (h + 1) * HEAD)
            s_v[h, lo:hi, :] = dot(k_v[lo:hi, cols], q_v[:, cols], NT)
            dp_v[h, lo:hi, :] = dot(v_v[lo:hi, cols], cot_v[:, cols], NT)
            for t in range(lo, hi, step):
                s = s_v[h, t : t + step, :] + bias[t : t + step, :]
                s_v[h, t : t + step, :] = s
                tops[h] = jnp.maximum(tops[h], jnp.max(s.reshape(step // 8, 8, ROWS), axis=0))

    def softmax_start(h, lo, hi, top):
        total = jnp.zeros((8, ROWS), F32)
        inner = jnp.zeros((8, ROWS), F32)
        for t in range(lo, hi, step):
            e = jnp.exp((s_v[h, t : t + step, :] - top) * SCALE)
            s_v[h, t : t + step, :] = e
            total += jnp.sum(e.reshape(step // 8, 8, ROWS), axis=0)
            inner += jnp.sum((e * dp_v[h, t : t + step, :]).reshape(step // 8, 8, ROWS), axis=0)
        return jnp.sum(total, axis=0, keepdims=True), jnp.sum(inner, axis=0, keepdims=True)

    products(0, ROWS)

    for b in range(4):
        lo, hi = ROWS + b * HALO, ROWS + (b + 1) * HALO
        if b == 3:
            early = [jnp.max(tops[h], axis=0, keepdims=True) for h in range(HEADS)]
            sums = [softmax_start(h, 0, lo, early[h]) for h in range(HEADS)]
        on_side(b, halo[lands[b]].wait_recv)
        if b in (1, 2):

            @pl.when(lat == (0 if b == 1 else 7))
            def _():
                ftab[lo:hi, :] = jnp.zeros((HALO, D), BF16)

        rows = ftab[lo:hi, :]
        k_v[lo:hi, :] = dot(rows, w_v[1]).astype(BF16)
        v_v[lo:hi, :] = dot(rows, w_v[2]).astype(BF16)
        products(lo, hi)

    last = TABLE - HALO
    for h in range(HEADS):
        cols = slice(h * HEAD, (h + 1) * HEAD)
        top = jnp.max(tops[h], axis=0, keepdims=True)
        fall = jnp.exp((early[h] - top) * SCALE)
        total, inner = softmax_start(h, last, TABLE, top)
        total += sums[h][0] * fall
        inner += sums[h][1] * fall
        inverse = 1.0 / total
        inner *= inverse
        fall *= inverse
        for t in range(0, TABLE, step):
            p = s_v[h, t : t + step, :] * (fall if t < last else inverse)
            p_v[h, t : t + step, :] = p.astype(BF16)
            ds_v[h, t : t + step, :] = (p * (dp_v[h, t : t + step, :] - inner) * SCALE).astype(BF16)
        gq_v[:, cols] = dot(ds_v[h], k_v[:, cols], TN).astype(BF16)
        if h < 2:
            gk_v[:, cols] = dot(ds_v[h], q_v[:, cols]).astype(BF16)

    def to_partner(c):
        for half in range(2):
            for y_hi in range(2):
                rows = jnp.concatenate(
                    [dw_v[pl.ds((c * 4 + zz) * 192 + y_hi * 96 + half * 48, 48), :] for zz in range(4)], axis=0
                )
                sorted_rows = dot(perm_v[...], rows)
                for k in range(8):
                    block = sorted_rows[k * 24 : (k + 1) * 24, :]
                    block = jnp.concatenate([block[:, 0:256], block[:, 256:512]], axis=0)
                    part[c, half, y_hi * 8 + k] = block.astype(BF16)
        copy = pltpu.make_async_remote_copy(
            src_ref=part.at[c, 1 - core],
            dst_ref=crecv.at[c],
            send_sem=cs_sem.at[c],
            recv_sem=cr_sem.at[c],
            device_id=partner,
            device_id_type=MESH,
        )
        copy.start()
        return copy

    def to_plane(c, from_partner):
        from_partner.wait_recv()
        copies = []
        for i, other in enumerate(planes):
            acc1[c, other] = (part[c, core, other].astype(F32) + crecv[c, other].astype(F32)).astype(BF16)
            copy = pltpu.make_async_remote_copy(
                src_ref=acc1.at[c, other],
                dst_ref=precv.at[c, i],
                send_sem=ps_sem.at[c, i],
                recv_sem=pr_sem.at[c, i],
                device_id=plane_peers[i],
                device_id_type=MESH,
            )
            copy.start()
            copies.append(copy)
        return copies

    def to_z(c, from_plane):
        total = part[c, core, plane].astype(F32) + crecv[c, plane].astype(F32)
        for i, copy in enumerate(from_plane):
            copy.wait_recv()
            total += precv[c, i].astype(F32)
        acc2[c, 0:24, :] = jnp.concatenate([total[0:24, :], total[24:48, :]], axis=1)
        acc2[c, 24:32, :] = jnp.zeros((8, D), F32)
        copies = []
        for zz in range(4):
            other = c * 4 + zz
            rows = acc2[c, zz * 6 : zz * 6 + 8, :]
            zsend[other] = jnp.concatenate([rows[:, 0:256], rows[:, 256:512]], axis=0).astype(BF16)
            copy = pltpu.make_async_remote_copy(
                src_ref=zsend.at[other],
                dst_ref=zrecv.at[z],
                send_sem=zs_sem.at[other],
                recv_sem=zr_sem.at[z],
                device_id=z_peers[other],
                device_id_type=MESH,
            )
            pl.when(z != other)(copy.start)
        return copies

    dw_v[0:D, :] = dot(gq_v[...], own, TN).astype(BF16)
    dw_v[D : D + 256, :] = dot(gk_v[:, 0:256], ftab[...], TN).astype(BF16)
    core_a = to_partner(0)
    for h in range(HEADS):
        cols = slice(h * HEAD, (h + 1) * HEAD)
        gv_v[:, cols] = dot(p_v[h], cot_v[:, cols]).astype(BF16)
        if h >= 2:
            gk_v[:, cols] = dot(ds_v[h], q_v[:, cols]).astype(BF16)
    plane_a = to_plane(0, core_a)
    dw_v[D + 256 : 2 * D, :] = dot(gk_v[:, 256:512], ftab[...], TN).astype(BF16)
    dw_v[2 * D : 3 * D, :] = dot(gv_v[...], ftab[...], TN).astype(BF16)
    core_b = to_partner(1)
    plane_b = to_plane(1, core_b)
    fg_own[...] = (
        dot(gq_v[...], w_v[0], NT) + dot(gk_v[0:ROWS, :], w_v[1], NT) + dot(gv_v[0:ROWS, :], w_v[2], NT)
    )

    back = []
    for b in range(4):
        back.append(
            pltpu.make_async_remote_copy(
                src_ref=fgh_s.at[b],
                dst_ref=fgh_r.at[pl.ds(lands[b] * HALO, HALO)],
                send_sem=rs_sem.at[b],
                recv_sem=rr_sem.at[lands[b]],
                device_id=sides[b],
                device_id_type=MESH,
            )
        )
    for b in (3, 1, 2, 0):
        on_side(b, halo[b].wait_send)
        rows = slice(ROWS + b * HALO, ROWS + (b + 1) * HALO)
        fgh_s[b] = (dot(gk_v[rows, :], w_v[1], NT) + dot(gv_v[rows, :], w_v[2], NT)).astype(BF16)
    for b in (1, 2, 0):
        on_side(b, back[b].start)
    to_z(0, plane_a)
    for b in (3,):
        on_side(b, back[b].start)
    to_z(1, plane_b)

    for b in range(4):
        on_side(lands[b], back[b].wait_recv)
        on_side(b, back[b].wait_send)

    @pl.when(lat == 0)
    def _():
        fgh_r[1 * HALO : 2 * HALO, :] = jnp.zeros((HALO, D), BF16)

    @pl.when(lat == 7)
    def _():
        fgh_r[2 * HALO : 3 * HALO, :] = jnp.zeros((HALO, D), BF16)

    fg_out[...] = (fg_own[...] + dot(picked[...], fgh_r[...])).astype(BF16)

    for copy in [core_a, core_b] + plane_a + plane_b:
        copy.wait_send()
    zrecv[z] = zsend[z]
    for other in range(8):
        copy = pltpu.make_async_remote_copy(
            src_ref=zsend.at[other],
            dst_ref=zrecv.at[other],
            send_sem=zs_sem.at[other],
            recv_sem=zr_sem.at[other],
            device_id=z_peers[other],
            device_id_type=MESH,
        )
        pl.when(z != other)(copy.wait)
    total = zrecv[0].astype(F32)
    for other in range(1, 8):
        total += zrecv[other].astype(F32)
    dw_out[...] = jnp.concatenate([total[0:6, :], total[8:14, :]], axis=1)


def sorting():
    source = np.arange(192).reshape(4, 8, 6).transpose(1, 0, 2).reshape(-1)
    return (source[:, None] == np.arange(192)[None, :]).astype(np.float32)


def shards(features, cotangent, w_query, w_key, w_value, neighbour, slot_mask, send_rows):
    whole = pl.BlockSpec(memory_space=VMEM)
    return pl.pallas_call(
        kernel,
        out_shape=(jax.ShapeDtypeStruct((ROWS, D), BF16), jax.ShapeDtypeStruct((6, D), F32)),
        in_specs=[pl.BlockSpec(memory_space=pl.ANY)] * 9,
        out_specs=(whole, whole),
        scratch_shapes=[
            VMEM((TABLE, D), BF16), VMEM((ROWS, D), BF16), VMEM((3, D, D), BF16), VMEM((SLOTS, ROWS), I32),
            VMEM((SLOTS, ROWS), I32), VMEM((4, HALO), I32), VMEM((192, 192), BF16),
            VMEM((ROWS, 4 * HALO), BF16), VMEM((ROWS, D), BF16), VMEM((TABLE, D), BF16), VMEM((TABLE, D), BF16),
            VMEM((TABLE, ROWS), F32), VMEM((HEADS, TABLE, ROWS), F32), VMEM((HEADS, TABLE, ROWS), F32),
            VMEM((HEADS, TABLE, ROWS), BF16), VMEM((HEADS, TABLE, ROWS), BF16),
            VMEM((ROWS, D), BF16), VMEM((TABLE, D), BF16), VMEM((TABLE, D), BF16), VMEM((3 * D, D), BF16),
            VMEM((2, 2, 16, 48, 256), BF16), VMEM((2, 16, 48, 256), BF16), VMEM((2, 16, 48, 256), BF16),
            VMEM((2, 15, 48, 256), BF16), VMEM((2, 32, D), F32), VMEM((8, 16, 256), BF16), VMEM((8, 16, 256), BF16),
            VMEM((ROWS, D), F32), VMEM((4, HALO, D), BF16), VMEM((4 * HALO, D), BF16),
            DMA((9,)), DMA((4,)), DMA((4,)), DMA((2,)), DMA((2,)), DMA((2, 15)), DMA((2, 15)),
            DMA((8,)), DMA((8,)), DMA((4,)), DMA((4,)),
        ],
        compiler_params=pltpu.CompilerParams(
            collective_id=0, has_side_effects=True, vmem_limit_bytes=60 * 1024 * 1024
        ),
        name="mesh_attention_backward",
    )(
        features, cotangent, w_query, w_key, w_value, neighbour.T, slot_mask.T, send_rows,
        jnp.asarray(sorting(), BF16),
    )


def solution(mesh):
    rows = P(("lon", "lat"), None)
    return jax.shard_map(
        shards,
        mesh=mesh,
        in_specs=(rows, rows, P(), P(), P(), rows, rows, rows),
        out_specs=(rows, rows),
        check_vma=False,
    )
```
